512 devices in a mesh: mem: 16 (over x, z_lo), tile: 32 (over y, z_hi, core).
Axes of the slice: x: 4, y: 4, z: 16 (z_hi: 4, z_lo: 4; z = z_hi * 4 + z_lo), core: 2. Of those that a mesh axis runs over, the one named last changes fastest.
Arguments:
- ensemble: bfloat16 [32, 256, 256, 256], P('mem', None, 'tile'), may hold values from -4 to 4
- control: float32 [32, 256, 256], P('mem', 'tile'), may hold values from -6 to 6
- weights: float32 [32], P('mem'), may hold values from 0.1 to 0.6
- member_band: int32 [32], P('mem'), may hold values from 0 to 3
- spread: float32 [4], replicated, may hold values from 0.05 to 0.24
- advect: float32 [2, 256], replicated, may hold values from -0.9 to 0.9
- damping: float32 [256], replicated, may hold values from 0.02 to 0.2
- innovation: float32 [256, 256, 256], P(None, 'tile'), may hold values from -4 to 4
- obs_weight: float32 [256, 256], P('tile'), may hold values from 0.3 to 27
Outputs:
- grad_control: float32 [32, 256, 256], P('mem', 'tile')
- grad_weight: float32 [32], P('mem')
The draws below stay inside these ranges and needn't reach their ends.
All inputs are finite; a program needn't handle non-finite values.
Results may differ from the reference program's by a relative error of at most 0.0003.
Values sent between devices are 32-bit elements; how exact they have to be, the bound alone decides.
No kernel may reach another device: no remote copies, remote signals or barrier semaphores. Data moves between devices by JAX's collectives and lax.ppermute only.
A program may use at most 64 MiB of HBM per device.

```python
import math
import jax
import jax.numpy as jnp
from jax import lax

VL = 256
NY = 256
SWEEPS = 8
BANDS = 4
M = 32
NX = 256


def draw_obs_weight(key, part):
    position = jnp.arange(NX, dtype=jnp.float32) / max(NX - 1, 1)
    ramp = jnp.exp(jnp.log(3.0) * position)
    noise = jax.random.uniform(key, (NX, NY), jnp.float32, 0.5, 2.0)
    return ramp[:, None] * noise


def touch_ends(drawn, stream_key, low, high):
    index_at = [jax.random.randint(jax.random.fold_in(stream_key, axis), (), 0, length) for axis, length in enumerate(drawn.shape)]
    longest = drawn.shape.index(max(drawn.shape))
    beside = index_at[:longest] + [(index_at[longest] + 1) % drawn.shape[longest]] + index_at[longest + 1:]
    return drawn.at[tuple(index_at)].set(low).at[tuple(beside)].set(high)


def levels(rng, dims, shards, smallest, largest):
    level, own = 1.0, jax.random.fold_in(rng, 6)
    for dim, shards_of in shards:
        steps = jnp.exp(jax.random.uniform(jax.random.fold_in(own, dim), (shards_of,), jnp.float32, smallest / len(shards), largest / len(shards)))
        level = level * jnp.repeat(steps, dims[dim] // shards_of).reshape([-1 if axis == dim else 1 for axis in range(len(dims))])
    return level


def bell_draw(own_key, shape, deviation, limit, shards=(), kind=jnp.bfloat16):
    drawn = jax.random.normal(own_key, shape, jnp.float32) * deviation
    if len(shards) > 0:
        drawn = levels(own_key, shape, shards, -0.22, 0.18) * drawn
    return jnp.clip(drawn, min=-limit, max=limit).astype(kind)


def setup_inputs(seed: int = 0) -> dict:
    seeds = jax.random.split(jax.random.key(seed), 10)
    return {
        "ensemble": bell_draw(seeds[0], (M, VL, NX, NY), 0.5, 4.0, ((0, 16), (2, 32))),
        "control": bell_draw(seeds[1], (M, NX, NY), 1.0, 6.0, ((0, 16), (1, 32)), jnp.float32),
        "weights": jnp.clip(0.1 + 0.5 * jax.random.uniform(seeds[2], (M,), jnp.float32) ** levels(seeds[2], (M,), ((0, 16),), -0.2, 0.2), 0.1, 0.6),
        "member_band": touch_ends(jax.random.randint(seeds[3], (M,), 0, BANDS), jax.random.fold_in(seeds[3], 1), 0, BANDS - 1).astype(jnp.int32),
        "spread": jnp.clip(jax.random.uniform(seeds[4], (BANDS,), jnp.float32, 0.05, 0.24), 0.05, 0.24),
        "advect": jnp.clip(jax.random.uniform(seeds[5], (2, VL), jnp.float32, -0.9, 0.9), -0.9, 0.9),
        "damping": jnp.clip(jax.random.uniform(seeds[6], (VL,), jnp.float32, 0.02, 0.2), 0.02, 0.2),
        "innovation": bell_draw(seeds[7], (VL, NX, NY), 0.5, 4.0, ((1, 32),), jnp.float32),
        "obs_weight": draw_obs_weight(jax.random.fold_in(seeds[9], 71), 0),
    }


def y_pairs(field):
    zero_col = jnp.zeros(field.shape[:-1] + (1,), field.dtype)
    north = jnp.concatenate([field[..., 1:], zero_col], axis=-1)
    south = jnp.concatenate([zero_col, field[..., :-1]], axis=-1)
    return (north, south)

def laplace(field):
    north, south = y_pairs(field)
    return jnp.roll(field, -1, -2) + jnp.roll(field, 1, -2) + north + south - 4.0 * field

def localize(field, rates):
    for sweep in range(SWEEPS):
        field = field + rates * laplace(field)
    return field

def dynamics(field, along_x, along_y, smooth):
    east = jnp.roll(field, -1, -2)
    west = jnp.roll(field, 1, -2)
    north, south = y_pairs(field)
    return field - along_x * ((east - west) * 0.5) - along_y * ((north - south) * 0.5) + smooth * (east + west + north + south - 4.0 * field)

def reference(ensemble, control, weights, member_band, spread, advect, damping, innovation, obs_weight):
    one_hot = (member_band[:, None] == jnp.arange(spread.shape[0], dtype=jnp.int32)[None, :]).astype(spread.dtype)
    rates = jnp.dot(one_hot, spread, precision=lax.Precision.HIGHEST)[:, None, None]
    localized = localize(control, rates)

    def accumulate(total, pair):
        member, field = pair
        return (total + member.astype(control.dtype) * field[None], None)
    scaled = weights[:, None, None] * localized
    increment, unused = lax.scan(accumulate, jnp.zeros(ensemble.shape[1:], control.dtype), (ensemble, scaled))
    along_x = advect[0][:, None, None]
    along_y = advect[1][:, None, None]
    smooth = damping[:, None, None]
    forward = dynamics(increment, along_x, along_y, smooth)
    weighted = obs_weight[None] * (forward - innovation)
    gradient = dynamics(weighted, -along_x, -along_y, smooth)

    def project(member):
        return lax.optimization_barrier(jnp.sum(member.astype(control.dtype) * gradient, axis=0))
    projected = lax.map(project, ensemble)
    grad_control = control + localize(weights[:, None, None] * projected, rates)
    grad_weight = lax.optimization_barrier(jnp.sum(localized * projected, axis=(1, 2))) / math.sqrt(NX * NY * VL)
    return (grad_control, grad_weight)
```

```python
import functools
import math

import jax
import jax.numpy as jnp
from jax import lax
from jax.experimental import pallas as pl
from jax.experimental.pallas import tpu as pltpu
from jax.sharding import Mesh
from jax.sharding import PartitionSpec as P

SWEEPS = 8
MEM = ("x", "zl")
TILE = ("y", "zh", "core")
T = 96
F32 = jnp.float32
SMEM = pl.BlockSpec(memory_space=pltpu.SMEM)
VMEM = pl.BlockSpec(memory_space=pltpu.VMEM)


def kernel_call(body, ins, outs, scratch=(), name=None):
    return pl.pallas_call(
        body,
        in_specs=[SMEM if s else VMEM for _, s in ins],
        out_specs=[SMEM if s else VMEM for _, s in outs],
        out_shape=[jax.ShapeDtypeStruct(shape, F32) for shape, _ in outs],
        scratch_shapes=list(scratch),
        compiler_params=pltpu.CompilerParams(vmem_limit_bytes=48 * 2**20),
        name=name,
    )(*[a for a, _ in ins])


def y_pair(field):
    lane = lax.broadcasted_iota(jnp.int32, field.shape, field.ndim - 1)
    last = field.shape[-1] - 1
    north = jnp.where(lane == last, 0.0, pltpu.roll(field, last, field.ndim - 1))
    south = jnp.where(lane == 0, 0.0, pltpu.roll(field, 1, field.ndim - 1))
    return north, south


def sweeps(field, rate):
    rows = field.shape[0]
    for _ in range(SWEEPS):
        north, south = y_pair(field)
        east = pltpu.roll(field, rows - 1, 0)
        west = pltpu.roll(field, 1, 0)
        field = field + rate * (east + west + north + south - 4.0 * field)
    return field[8:16]


def strips(core, own, near, far):
    first = core == 0
    above = jnp.where(first, far, near)
    below = jnp.where(first, near, far)
    return jnp.concatenate([above, own, below], axis=0)


def start_kernel(s_planes, pos, band, spread, weights, control, near, far, ens, loc_o, pay_o):
    core = pos[2]
    s4 = s_planes // 4
    scaled = []
    for m in range(2):
        ext = strips(core, control[m], near[8 * m : 8 * m + 8], far[8 * m : 8 * m + 8])
        loc = sweeps(ext, spread[band[m]])
        loc_o[m] = loc
        scaled.append(weights[m] * loc)
        for x in range(4):
            pay_o[x, s4 + m] = scaled[m]
    step = 8 if s4 % 8 == 0 else 4
    for x in range(4):

        def body(i, _, x=x):
            j = pl.multiple_of(i * step, step)
            a = ens[0, pl.ds(x * s4 + j, step)].astype(F32) * scaled[0][None]
            b = ens[1, pl.ds(x * s4 + j, step)].astype(F32) * scaled[1][None]
            pay_o[x, pl.ds(j, step)] = a + b
            return 0

        lax.fori_loop(0, s4 // step, body, 0)


def mid_kernel(s_planes, t_planes, r1, g, pay_o):
    s4, t4 = s_planes // 4, t_planes // 4
    s16, t16 = s4 // 4, t4 // 4
    for z in range(4):
        for j in range(s16):
            k = z * s16 + j
            pay_o[z, j] = (r1[0, k] + r1[1, k]) + (r1[2, k] + r1[3, k])
    scaled = [r1[x, s4 + m] for x in range(4) for m in range(2)]
    for z in range(4):
        for j in range(t16):
            k = z * t16 + j
            pay_o[z, s16 + j] = sum(
                g[x, m, k] * scaled[2 * x + m] for x in range(4) for m in range(2)
            )


def edge_kernel(pos, r2, inc_o, near_o, far_o):
    first = pos[2] == 0
    inc = (r2[0] + r2[1]) + (r2[2] + r2[3])
    inc_o[...] = inc
    head, tail = inc[:, 0:2], inc[:, 6:8]
    near_o[...] = jnp.where(first, tail, head)
    far_o[...] = jnp.where(first, head, tail)


def dynamics_kernel(
    s_planes, t_planes, pos, advect, damping, inc, near, far, innov, obsw, near0, far0,
    grad_o, fields, misfit, seen, weight,
):
    x, z, core = pos[0], pos[1], pos[2]
    first = core == 0
    s16, t16 = s_planes // 16, t_planes // 16
    fields[:, 8:16] = inc[...]
    fields[:, 6:8] = jnp.where(first, far[...], near[...])
    fields[:, 16:18] = jnp.where(first, near[...], far[...])
    seen[:, 8:16] = innov[...]
    above = jnp.where(first, far0[16:32], near0[16:32])
    below = jnp.where(first, near0[16:32], far0[16:32])
    for p in range(16):
        seen[p, 7:8] = above[p : p + 1]
        seen[p, 16:17] = below[p : p + 1]
    weight[8:16] = obsw[...]
    weight[7:8] = jnp.where(first, far0[32:33], near0[32:33])
    weight[16:17] = jnp.where(first, near0[32:33], far0[32:33])
    for p in range(16):
        if p < s16:
            k = (x * 4 + z) * s16 + p
        else:
            k = s_planes + (x * 4 + z) * t16 + (p - s16)
        a, b, e = advect[0, k], advect[1, k], damping[k]
        center, east, west = fields[p, 7:17], fields[p, 8:18], fields[p, 6:16]
        north, south = y_pair(center)
        forward = (
            center
            - a * ((east - west) * 0.5)
            - b * ((north - south) * 0.5)
            + e * (east + west + north + south - 4.0 * center)
        )
        misfit[p, 7:17] = weight[7:17] * (forward - seen[p, 7:17])
        center, east, west = misfit[p, 8:16], misfit[p, 9:17], misfit[p, 7:15]
        north, south = y_pair(center)
        grad_o[p] = (
            center
            + a * ((east - west) * 0.5)
            + b * ((north - south) * 0.5)
            + e * (east + west + north + south - 4.0 * center)
        )


def back_kernel(s_planes, t_planes, g64, g, pay_o):
    s4, t4 = s_planes // 4, t_planes // 4
    s16, t16 = s4 // 4, t4 // 4
    for z in range(4):
        for j in range(s16):
            plane = g64[z, j]
            for x in range(4):
                pay_o[x, z * s16 + j] = plane
    for x in range(4):
        for m in range(2):
            total = None
            for z in range(4):
                part = jnp.sum(g[x, m, z * t16 : (z + 1) * t16] * g64[z, s16:], axis=0)
                total = part if total is None else total + part
            pay_o[x, s4 + m] = total


def project_kernel(s_planes, weights, r3, ens, loc, send_o, sums_o):
    s4 = s_planes // 4
    step = 8 if s4 % 8 == 0 else 4
    totals = []
    for m in range(2):
        totals.append((r3[0, s4 + m] + r3[1, s4 + m]) + (r3[2, s4 + m] + r3[3, s4 + m]))
    for x in range(4):

        def body(i, carry, x=x):
            j = pl.multiple_of(i * step, step)
            grad = r3[x, pl.ds(j, step)]
            return tuple(
                carry[m] + jnp.sum(ens[m, pl.ds(x * s4 + j, step)].astype(F32) * grad, axis=0)
                for m in range(2)
            )

        totals = lax.fori_loop(0, s4 // step, body, tuple(totals))
    for m in range(2):
        send_o[m] = weights[m] * totals[m]
        cells = jnp.sum(loc[m] * totals[m], axis=0, keepdims=True)
        sums_o[:, m : m + 1] = jnp.broadcast_to((cells[:, :128] + cells[:, 128:])[None], (32, 1, 128))


def end_kernel(scale, pos, band, spread, control, send, near, far, sums, out_o, weight_o):
    core = pos[2]
    for m in range(2):
        out_o[m] = control[m] + sweeps(strips(core, send[m], near[m], far[m]), spread[band[m]])
    total = jnp.sum(sums[...], axis=0)
    for m in range(2):
        weight_o[m] = jnp.sum(total[m : m + 1]) * scale


def swap(near, far):
    n = 32
    far_pairs = [(i, (i + 1) % n if i % 2 else (i - 1) % n) for i in range(n)]
    far = lax.ppermute(far, TILE, far_pairs)
    near = lax.ppermute(near, TILE, [(i, i ^ 1) for i in range(n)])
    return near, far


def per_device(
    ensemble, control, weights, member_band, spread, advect, damping, innovation, obs_weight
):
    t, s = T, ensemble.shape[1] - T
    s4, t4, s16, t16 = s // 4, t // 4, s // 16, t // 16
    ix, iz, core = lax.axis_index("x"), lax.axis_index("zl"), lax.axis_index("core")
    pos = jnp.stack([ix, iz, core]).astype(jnp.int32)
    own = ix * 4 + iz

    moved = ensemble[:, s:].astype(F32).reshape(2, 4, t4, 8, 256)
    moved = lax.optimization_barrier(jnp.moveaxis(moved, 1, 0))
    g = lax.all_to_all(moved, "x", 0, 0, tiled=True)

    def edges(row):
        return [
            lax.dynamic_slice(innovation, (own * s16, row, 0), (s16, 1, 256)).reshape(s16, 256),
            lax.dynamic_slice(innovation, (s + own * t16, row, 0), (t16, 1, 256)).reshape(t16, 256),
            lax.dynamic_slice(obs_weight, (row, 0), (1, 256)),
        ]

    strip = control.reshape(16, 256)
    near_row = jnp.where(core == 0, 7, 0)
    near0, far0 = swap(
        jnp.concatenate([strip, *edges(near_row)]), jnp.concatenate([strip, *edges(7 - near_row)])
    )
    loc, pay1 = kernel_call(
        functools.partial(start_kernel, s),
        [(pos, 1), (member_band, 1), (spread, 1), (weights, 1), (control, 0), (near0, 0), (far0, 0), (ensemble, 0)],
        [((2, 8, 256), 0), ((4, s4 + 2, 8, 256), 0)],
        name="start",
    )
    r1 = lax.all_to_all(pay1, "x", 0, 0, tiled=True)
    (pay2,) = kernel_call(
        functools.partial(mid_kernel, s, t), [(r1, 0), (g, 0)], [((4, 16, 8, 256), 0)], name="mid"
    )
    r2 = lax.all_to_all(pay2, "zl", 0, 0, tiled=True)
    inc, near, far = kernel_call(
        edge_kernel, [(pos, 1), (r2, 0)],
        [((16, 8, 256), 0), ((16, 2, 256), 0), ((16, 2, 256), 0)], name="edge",
    )
    near, far = swap(near, far)
    seen = jnp.concatenate(
        [
            lax.dynamic_slice_in_dim(innovation, own * s16, s16, 0),
            lax.dynamic_slice_in_dim(innovation, s + own * t16, t16, 0),
        ]
    )
    (grad,) = kernel_call(
        functools.partial(dynamics_kernel, s, t),
        [(pos, 1), (advect, 1), (damping, 1), (inc, 0), (near, 0), (far, 0), (seen, 0), (obs_weight, 0), (near0, 0), (far0, 0)],
        [((16, 8, 256), 0)],
        [pltpu.VMEM((16, 24, 256), F32)] * 3 + [pltpu.VMEM((24, 256), F32)],
        name="dynamics",
    )
    g64 = lax.all_gather(grad, "zl", axis=0, tiled=False)
    (pay3,) = kernel_call(
        functools.partial(back_kernel, s, t),
        [(g64, 0), (g, 0)], [((4, s4 + 2, 8, 256), 0)], name="back",
    )
    r3 = lax.all_to_all(pay3, "x", 0, 0, tiled=True)
    send, sums = kernel_call(
        functools.partial(project_kernel, s),
        [(weights, 1), (r3, 0), (ensemble, 0), (loc, 0)],
        [((2, 8, 256), 0), ((32, 2, 128), 0)], name="project",
    )
    near, far = swap(send, send)
    sums = lax.all_to_all(sums, TILE, 0, 0, tiled=True)
    cells = 32 * control.shape[1] * control.shape[2] * ensemble.shape[1]
    return tuple(
        kernel_call(
            functools.partial(end_kernel, 1.0 / math.sqrt(cells)),
            [(pos, 1), (member_band, 1), (spread, 1), (control, 0), (send, 0), (near, 0), (far, 0), (sums, 0)],
            [((2, 8, 256), 0), ((2,), 1)], name="end",
        )
    )


def solution(mesh):
    mesh = Mesh(mesh.devices.reshape(4, 4, 4, 4, 2), MEM + TILE)
    in_specs = (
        P(MEM, None, TILE, None),
        P(MEM, TILE, None),
        P(MEM),
        P(MEM),
        P(),
        P(),
        P(),
        P(None, TILE, None),
        P(TILE, None),
    )
    out_specs = (P(MEM, TILE, None), P(MEM))
    return jax.shard_map(
        per_device, mesh=mesh, in_specs=in_specs, out_specs=out_specs, check_vma=False
    )
```

```python
import functools
import math

import jax
import jax.numpy as jnp
from jax import lax
from jax.experimental import pallas as pl
from jax.experimental.pallas import tpu as pltpu
from jax.sharding import Mesh
from jax.sharding import PartitionSpec as P

SWEEPS = 8
AXES = ("x", "zp", "zq", "y", "zh", "core")
MEM = ("x", "zp", "zq")
GROUP = ("x", "zq")
TILE = ("y", "zh", "core")
F32 = jnp.float32


def smem():
    return pl.BlockSpec(memory_space=pltpu.SMEM)


def whole(shape):
    return pl.BlockSpec(shape, lambda *i: (0,) * len(shape))


def call(body, name, grid, ins, outs, scratch=(), vmem=40 * 2**20):
    return pl.pallas_call(
        body,
        grid=grid,
        in_specs=[s for _, s in ins],
        out_specs=[s for _, s in outs],
        out_shape=[jax.ShapeDtypeStruct(shape, F32) for shape, _ in outs],
        scratch_shapes=list(scratch),
        compiler_params=pltpu.CompilerParams(vmem_limit_bytes=vmem),
        name=name,
    )(*[a for a, _ in ins])


def y_pair(field):
    lane = lax.broadcasted_iota(jnp.int32, field.shape, field.ndim - 1)
    last = field.shape[-1] - 1
    north = jnp.where(lane == last, 0.0, pltpu.roll(field, last, field.ndim - 1))
    south = jnp.where(lane == 0, 0.0, pltpu.roll(field, 1, field.ndim - 1))
    return north, south


def sweeps(field, rate):
    rows = field.shape[0]
    for _ in range(SWEEPS):
        north, south = y_pair(field)
        east = pltpu.roll(field, rows - 1, 0)
        west = pltpu.roll(field, 1, 0)
        field = field + rate * (east + west + north + south - 4.0 * field)
    return field[8:16]


def strips(first, own, near, far):
    above = jnp.where(first, far, near)
    below = jnp.where(first, near, far)
    return jnp.concatenate([above, own, below], axis=0)


def bring_kernel(ens, control, ens_o, control_o, sem):
    copies = [
        pltpu.make_async_copy(ens, ens_o, sem.at[0]),
        pltpu.make_async_copy(control, control_o, sem.at[1]),
    ]
    for copy in copies:
        copy.start()
    for copy in copies:
        copy.wait()


def start_kernel(pos, scal, control, far, near, ens, loc_o, part_o):
    scaled = []
    for m in range(2):
        loc = sweeps(strips(pos[0] == 0, control[m], near[m], far[m]), scal[m])
        loc_o[m] = loc
        scaled.append(scal[2 + m] * loc)
    n = part_o.shape[1]
    for b in range(8):
        slot = lax.bitwise_xor(jnp.int32(b), pos[2])
        for j in range(0, n, 8):
            k = b * n + j
            part_o[slot, j : j + 8] = (
                ens[0, k : k + 8].astype(F32) * scaled[0][None]
                + ens[1, k : k + 8].astype(F32) * scaled[1][None]
            )


def tree(parts):
    while len(parts) > 1:
        parts = [p + q for p, q in zip(parts[::2], parts[1::2])]
    return parts[0]


def mid_kernel(parts, sum_o):
    n = sum_o.shape[0]
    for j in range(0, n, 4):
        sum_o[j : j + 4] = tree([parts[b, j : j + 4] for b in range(8)])


def edge_kernel(pos, keep, got, seen, obsw, inc_o, far_o, near_o):
    first = pos[0] == 0
    n = inc_o.shape[0]
    for p in range(n):
        inc = keep[p] + got[p]
        inc_o[p] = inc
        see = seen[p]
        head = (inc[0:1], inc[1:2], see[0:1])
        tail = (inc[6:7], inc[7:8], see[7:8])
        for j in range(3):
            near_o[n * j + p : n * j + p + 1] = jnp.where(first, tail[j], head[j])
            far_o[n * j + p : n * j + p + 1] = jnp.where(first, head[j], tail[j])
    head, tail = obsw[0:1], obsw[7:8]
    near_o[3 * n : 3 * n + 1] = jnp.where(first, tail, head)
    far_o[3 * n : 3 * n + 1] = jnp.where(first, head, tail)


def dynamics_kernel(pos, advect, damping, inc, far, near, seen, obsw, out, fields, misfit, see, weight):
    n = inc.shape[0]

    first = pos[0] == 0
    fields[:, 8:16] = inc[...]
    see[:, 8:16] = seen[...]
    above = jnp.where(first, far[...], near[...])
    below = jnp.where(first, near[...], far[...])
    weight[8:16] = obsw[...]
    weight[7:8] = above[3 * n : 3 * n + 1]
    weight[16:17] = below[3 * n : 3 * n + 1]
    own = pos[1]
    for p in range(n):
        k = own * n + p
        fields[p, 6:7] = above[p : p + 1]
        fields[p, 7:8] = above[n + p : n + 1 + p]
        see[p, 7:8] = above[2 * n + p : 2 * n + 1 + p]
        fields[p, 16:17] = below[p : p + 1]
        fields[p, 17:18] = below[n + p : n + 1 + p]
        see[p, 16:17] = below[2 * n + p : 2 * n + 1 + p]
        ax, ay, e = advect[0, k], advect[1, k], damping[k]
        center, east, west = fields[p, 7:17], fields[p, 8:18], fields[p, 6:16]
        north, south = y_pair(center)
        forward = (
            center
            - ax * ((east - west) * 0.5)
            - ay * ((north - south) * 0.5)
            + e * (east + west + north + south - 4.0 * center)
        )
        misfit[p, 7:17] = weight[7:17] * (forward - see[p, 7:17])
        center, east, west = misfit[p, 8:16], misfit[p, 9:17], misfit[p, 7:15]
        north, south = y_pair(center)
        grad = (
            center
            + ax * ((east - west) * 0.5)
            + ay * ((north - south) * 0.5)
            + e * (east + west + north + south - 4.0 * center)
        )
        for b in range(8):
            out[b, p] = grad


def project_kernel(pos, scal, grad, ens, loc, send_o, sums_o, total):
    step = pl.program_id(0)
    n = grad.shape[1]

    @pl.when(step == 0)
    def _():
        total[...] = jnp.zeros_like(total)

    first = lax.bitwise_xor(step, pos[2]) * n
    for m in range(2):
        parts = [
            jnp.sum(ens[m, pl.ds(first + j, 8)].astype(F32) * grad[0, j : j + 8], axis=0)
            for j in range(0, n, 8)
        ]
        total[m] += tree(parts)

    @pl.when(step == pl.num_programs(0) - 1)
    def _():
        for m in range(2):
            send_o[m] = scal[2 + m] * total[m]
            cells = jnp.sum(loc[m] * total[m], axis=0, keepdims=True)
            cells = cells[:, :128] + cells[:, 128:]
            sums_o[:, m : m + 1] = jnp.broadcast_to(cells[None], (32, 1, 128))


def end_kernel(scale, pos, scal, control, send, far, near, sums, out_o, weight_o):
    for m in range(2):
        out_o[m] = control[m] + sweeps(strips(pos[0] == 0, send[m], near[m], far[m]), scal[m])
    total = jnp.sum(sums[...], axis=0)
    for m in range(2):
        weight_o[m] = jnp.sum(total[m : m + 1]) * scale


def swap_tiles(near, far):
    n = 32
    far_pairs = [(i, (i + 1) % n if i % 2 else (i - 1) % n) for i in range(n)]
    far = lax.ppermute(far, TILE, far_pairs)
    near = lax.ppermute(near, TILE, [(i, i ^ 1) for i in range(n)])
    return near, far


def per_device(
    ensemble, control, weights, member_band, spread, advect, damping, innovation, obs_weight
):
    n = ensemble.shape[1] // 8
    ix, zp, zq, core = (lax.axis_index(a) for a in ("x", "zp", "zq", "core"))
    own = ix * 2 + lax.bitwise_xor(zp, zq)
    pos = jnp.stack([core, own, zp]).astype(jnp.int32)
    one_hot = member_band[:, None] == jnp.arange(spread.shape[0], dtype=jnp.int32)[None, :]
    rates = jnp.sum(jnp.where(one_hot, spread[None], 0.0), axis=1)
    scal = jnp.concatenate([rates, weights])
    strip2, planes, rows = (2, 8, 256), (n, 8, 256), (3 * n + 1, 256)
    w2, wn, w4, row_spec = whole(strip2), whole(planes), whole((4, 8, 256)), whole(rows)
    strip_spec = whole((8, 256))

    hbm = pl.BlockSpec(memory_space=pltpu.HBM)
    vmem = pl.BlockSpec(memory_space=pltpu.VMEM)
    ens, own_control = pl.pallas_call(
        bring_kernel,
        in_specs=[hbm, hbm],
        out_specs=[vmem, vmem],
        out_shape=[jax.ShapeDtypeStruct(a.shape, a.dtype) for a in (ensemble, control)],
        scratch_shapes=[pltpu.SemaphoreType.DMA((2,))],
        compiler_params=pltpu.CompilerParams(vmem_limit_bytes=40 * 2**20),
        name="bring",
    )(ensemble, control)
    near0, far0 = swap_tiles(control, control)
    loc, parts = call(
        start_kernel, "start", (1,),
        [(pos, smem()), (scal, smem()), (own_control, w2), (far0, w2), (near0, w2), (ens, whole(ens.shape))],
        [(strip2, w2), ((8, n, 8, 256), whole((8, n, 8, 256)))],
    )
    parts = lax.all_to_all(parts, GROUP, 0, 0, tiled=True)
    (part,) = call(mid_kernel, "mid", (1,), [(parts, whole(parts.shape))], [(planes, wn)])
    got = lax.ppermute(part, ("zp", "zq"), [(0, 3), (3, 0), (1, 2), (2, 1)])
    seen = lax.dynamic_slice_in_dim(innovation, own * n, n, 0)
    inc, far, near = call(
        edge_kernel, "edge", (1,),
        [(pos, smem()), (part, wn), (got, wn), (seen, wn), (obs_weight, strip_spec)],
        [(planes, wn), (rows, row_spec), (rows, row_spec)],
    )
    near, far = swap_tiles(near, far)
    (grad,) = call(
        dynamics_kernel, "dynamics", (1,),
        [(pos, smem()), (advect, smem()), (damping, smem()), (inc, wn), (far, row_spec),
         (near, row_spec), (seen, wn), (obs_weight, strip_spec)],
        [((8, n, 8, 256), whole((8, n, 8, 256)))],
        [pltpu.VMEM((n, 24, 256), F32)] * 3 + [pltpu.VMEM((24, 256), F32)],
    )
    grad = lax.all_to_all(grad, GROUP, 0, 0, tiled=True)
    send, sums = call(
        project_kernel, "project", (8,),
        [(pos, smem()), (scal, smem()),
         (grad, pl.BlockSpec((1, n, 8, 256), lambda b: (b, 0, 0, 0))),
         (ensemble, whole(ensemble.shape)), (loc, w2)],
        [(strip2, w2), ((32, 2, 128), whole((32, 2, 128)))],
        [pltpu.VMEM(strip2, F32)],
    )
    near, far = swap_tiles(send, send)
    sums = lax.all_to_all(sums, TILE, 0, 0, tiled=True)
    cells = 32 * control.shape[1] * control.shape[2] * ensemble.shape[1]
    return tuple(
        call(
            functools.partial(end_kernel, 1.0 / math.sqrt(cells)), "end", (1,),
            [(pos, smem()), (scal, smem()), (control, w2), (send, w2), (far, w2), (near, w2),
             (sums, whole(sums.shape))],
            [(strip2, w2), ((2,), smem())],
        )
    )


def solution(mesh):
    mesh = Mesh(mesh.devices.reshape(4, 2, 2, 4, 4, 2), AXES)
    in_specs = (
        P(MEM, None, TILE, None),
        P(MEM, TILE, None),
        P(MEM),
        P(MEM),
        P(),
        P(),
        P(),
        P(None, TILE, None),
        P(TILE, None),
    )
    out_specs = (P(MEM, TILE, None), P(MEM))
    return jax.shard_map(
        per_device, mesh=mesh, in_specs=in_specs, out_specs=out_specs, check_vma=False
    )
```

```python
import functools
import math

import jax
import jax.numpy as jnp
from jax import lax
from jax.experimental import pallas as pl
from jax.experimental.pallas import tpu as pltpu
from jax.sharding import Mesh
from jax.sharding import PartitionSpec as P

SWEEPS = 8
AXES = ("x", "zp", "zq", "y", "zh", "core")
MEM = ("x", "zp", "zq")
GROUP = ("x", "zq")
TILE = ("y", "zh", "core")
F32 = jnp.float32


def smem():
    return pl.BlockSpec(memory_space=pltpu.SMEM)


def whole(shape):
    return pl.BlockSpec(shape, lambda *i: (0,) * len(shape))


def call(body, name, grid, ins, outs, scratch=(), vmem=40 * 2**20):
    return pl.pallas_call(
        body,
        grid=grid,
        in_specs=[s for _, s in ins],
        out_specs=[s for _, s in outs],
        out_shape=[jax.ShapeDtypeStruct(shape, F32) for shape, _ in outs],
        scratch_shapes=list(scratch),
        compiler_params=pltpu.CompilerParams(vmem_limit_bytes=vmem),
        name=name,
    )(*[a for a, _ in ins])


def y_pair(field):
    lane = lax.broadcasted_iota(jnp.int32, field.shape, field.ndim - 1)
    last = field.shape[-1] - 1
    north = jnp.where(lane == last, 0.0, pltpu.roll(field, last, field.ndim - 1))
    south = jnp.where(lane == 0, 0.0, pltpu.roll(field, 1, field.ndim - 1))
    return north, south


def rate_of(pos, scal, m):
    rate = scal[2]
    for b in range(1, scal.shape[0] - 2):
        rate = jnp.where(pos[3 + m] == b, scal[2 + b], rate)
    return rate


def sweeps(field, rate):
    rows = field.shape[0]
    for _ in range(SWEEPS):
        north, south = y_pair(field)
        east = pltpu.roll(field, rows - 1, 0)
        west = pltpu.roll(field, 1, 0)
        field = field + rate * (east + west + north + south - 4.0 * field)
    return field[8:16]


def strips(first, own, near, far):
    above = jnp.where(first, far, near)
    below = jnp.where(first, near, far)
    return jnp.concatenate([above, own, below], axis=0)


def bring_kernel(ens, control, ens_o, control_o, sem):
    copies = [
        pltpu.make_async_copy(ens, ens_o, sem.at[0]),
        pltpu.make_async_copy(control, control_o, sem.at[1]),
    ]
    for copy in copies:
        copy.start()
    for copy in copies:
        copy.wait()


def start_kernel(pos, scal, control, far, near, ens, loc_o, part_o):
    scaled = []
    for m in range(2):
        loc = sweeps(strips(pos[0] == 0, control[m], near[m], far[m]), rate_of(pos, scal, m))
        loc_o[m] = loc
        scaled.append(scal[m] * loc)
    n = part_o.shape[1]
    for b in range(8):
        slot = lax.bitwise_xor(jnp.int32(b), pos[2])
        for j in range(0, n, 8):
            k = b * n + j
            part_o[slot, j : j + 8] = (
                ens[0, k : k + 8].astype(F32) * scaled[0][None]
                + ens[1, k : k + 8].astype(F32) * scaled[1][None]
            )


def tree(parts):
    while len(parts) > 1:
        parts = [p + q for p, q in zip(parts[::2], parts[1::2])]
    return parts[0]


def mid_kernel(parts, edge_o, inner_o):
    half = edge_o.shape[0]
    low = lax.broadcasted_iota(jnp.int32, edge_o.shape[1:], 0) < 4
    for p in range(half):
        one, two = (pltpu.roll(tree([parts[b, k] for b in range(8)]), 2, 0) for k in (p, p + half))
        edge_o[p] = jnp.where(low, one, pltpu.roll(two, 4, 0))
        inner_o[p] = jnp.where(low, pltpu.roll(one, 4, 0), two)


def edge_kernel(pos, coef, keep, got, seen, obsw, edge_o, far_o, near_o, rows):
    first = pos[0] == 0
    n = seen.shape[0]
    half = n // 2
    for p in range(half):
        edge = keep[p] + got[p]
        edge_o[p] = edge
        for j in range(4):
            row = (j + 2) % 4
            rows[row, p : p + 1] = edge[j : j + 1]
            rows[row, half + p : half + p + 1] = edge[j + 4 : j + 5]
    for p in range(n):
        rows[4, p : p + 1] = seen[p, 0:1]
        rows[5, p : p + 1] = seen[p, 7:8]
    a, b, e = coef[:, 0:1], coef[:, 1:2], coef[:, 2:3]

    def without(center, beside, sign, weight, see):
        north, south = y_pair(center)
        forward = (
            center
            - sign * a * (beside * 0.5)
            - b * ((north - south) * 0.5)
            + e * (beside + north + south - 4.0 * center)
        )
        return weight * (forward - see)

    head = (rows[0], without(rows[0], rows[1], 1.0, obsw[0:1], rows[4]), obsw[0:1])
    tail = (rows[3], without(rows[3], rows[2], -1.0, obsw[7:8], rows[5]), obsw[7:8])
    for j, (lo, hi) in enumerate(((0, n), (n, 2 * n), (2 * n, 2 * n + 1))):
        near_o[lo:hi] = jnp.where(first, tail[j], head[j])
        far_o[lo:hi] = jnp.where(first, head[j], tail[j])


def dynamics_kernel(pos, advect, damping, edge, inner, got, far, near, seen, obsw, out, above, below, inc):
    n = seen.shape[0]
    half = n // 2
    low = lax.broadcasted_iota(jnp.int32, edge.shape[1:], 0) < 4
    for p in range(half):
        outer, middle = edge[p], inner[p] + got[p]
        inc[p] = pltpu.roll(jnp.where(low, outer, pltpu.roll(middle, 4, 0)), 6, 0)
        inc[half + p] = pltpu.roll(jnp.where(low, pltpu.roll(outer, 4, 0), middle), 6, 0)
    first = pos[0] == 0
    above[...] = jnp.where(first, far[...], near[...])
    below[...] = jnp.where(first, near[...], far[...])
    weight = obsw[...]
    row = lax.broadcasted_iota(jnp.int32, weight.shape, 0)
    top, bottom = row == 0, row == weight.shape[0] - 1
    weight_above = jnp.broadcast_to(above[2 * n : 2 * n + 1], weight.shape)
    weight_below = jnp.broadcast_to(below[2 * n : 2 * n + 1], weight.shape)

    def pairs(field, over, under):
        east = jnp.where(bottom, under, pltpu.roll(field, field.shape[0] - 1, 0))
        west = jnp.where(top, over, pltpu.roll(field, 1, 0))
        north, south = y_pair(field)
        return east, west, north, south

    for p in range(n):
        k = pos[1] * n + p
        ax, ay, e = advect[0, k], advect[1, k], damping[k]
        center = inc[p]
        east, west, north, south = pairs(center, above[p : p + 1], below[p : p + 1])
        forward = (
            center
            - ax * ((east - west) * 0.5)
            - ay * ((north - south) * 0.5)
            + e * (east + west + north + south - 4.0 * center)
        )
        misfit = weight * (forward - seen[p])
        over = above[n + p : n + p + 1] + weight_above * ((e - 0.5 * ax) * center)
        under = below[n + p : n + p + 1] + weight_below * ((e + 0.5 * ax) * center)
        east, west, north, south = pairs(misfit, over, under)
        grad = (
            misfit
            + ax * ((east - west) * 0.5)
            + ay * ((north - south) * 0.5)
            + e * (east + west + north + south - 4.0 * misfit)
        )
        for b in range(8):
            out[b, p] = grad


def project_kernel(pos, scal, grad, ens, loc, send_o, sums_o):
    n = grad.shape[1]
    for m in range(2):
        parts = []
        for slot in range(8):
            first = lax.bitwise_xor(jnp.int32(slot), pos[2]) * n
            for j in range(0, n, 8):
                parts.append(
                    jnp.sum(
                        ens[m, pl.ds(first + j, 8)].astype(F32) * grad[slot, j : j + 8], axis=0
                    )
                )
            parts = [tree(parts[:4]), *parts[4:]] if slot == 0 else [parts[0] + tree(parts[1:])]
        total = parts[0]
        send_o[m] = scal[m] * total
        cells = jnp.sum(loc[m] * total, axis=0, keepdims=True)
        cells = cells[:, :128] + cells[:, 128:]
        sums_o[:, m : m + 1] = jnp.broadcast_to(cells[None], (32, 1, 128))


def end_kernel(scale, pos, scal, control, send, near, far, sums, out_o, weight_o):
    for m in range(2):
        out_o[m] = control[m] + sweeps(
            strips(pos[0] == 0, send[m], near[m], far[m]), rate_of(pos, scal, m)
        )
    total = jnp.sum(sums[...], axis=0)
    for m in range(2):
        weight_o[m] = jnp.sum(total[m : m + 1]) * scale


def swap_tiles(near, far):
    n = 32
    far_pairs = [(i, (i + 1) % n if i % 2 else (i - 1) % n) for i in range(n)]
    far = lax.ppermute(far, TILE, far_pairs)
    near = lax.ppermute(near, TILE, [(i, i ^ 1) for i in range(n)])
    return near, far


def per_device(
    ensemble, control, weights, member_band, spread, advect, damping, innovation, obs_weight
):
    n = ensemble.shape[1] // 8
    ix, zp, zq, core = (lax.axis_index(a) for a in ("x", "zp", "zq", "core"))
    own = ix * 2 + lax.bitwise_xor(zp, zq)
    pos = jnp.concatenate([jnp.stack([core, own, zp]).astype(jnp.int32), member_band])
    scal = jnp.concatenate([weights, spread])
    strip2, planes, rows = (2, 8, 256), (n, 8, 256), (2 * n + 1, 256)
    w2, wn, w4, row_spec = whole(strip2), whole(planes), whole((4, 8, 256)), whole(rows)
    strip_spec = whole((8, 256))

    hbm = pl.BlockSpec(memory_space=pltpu.HBM)
    vmem = pl.BlockSpec(memory_space=pltpu.VMEM)
    ens, own_control = pl.pallas_call(
        bring_kernel,
        in_specs=[hbm, hbm],
        out_specs=[vmem, vmem],
        out_shape=[jax.ShapeDtypeStruct(a.shape, a.dtype) for a in (ensemble, control)],
        scratch_shapes=[pltpu.SemaphoreType.DMA((2,))],
        compiler_params=pltpu.CompilerParams(vmem_limit_bytes=40 * 2**20),
        name="bring",
    )(ensemble, control)
    near0, far0 = swap_tiles(control, control)
    loc, parts = call(
        start_kernel, "start", (1,),
        [(pos, smem()), (scal, smem()), (own_control, w2), (far0, w2), (near0, w2), (ens, whole(ens.shape))],
        [(strip2, w2), ((8, n, 8, 256), whole((8, n, 8, 256)))],
    )
    parts, offset = lax.optimization_barrier((parts, (own * n).astype(jnp.uint32)))
    parts = lax.all_to_all(parts, GROUP, 0, 0, tiled=True)
    halves, wh = (n // 2, 8, 256), whole((n // 2, 8, 256))
    edge, inner = call(
        mid_kernel, "mid", (1,), [(parts, whole(parts.shape))], [(halves, wh), (halves, wh)]
    )
    across = [(0, 3), (3, 0), (1, 2), (2, 1)]
    got_edge = lax.ppermute(edge, ("zp", "zq"), across)
    got_inner = lax.ppermute(inner, ("zp", "zq"), across)
    zero = jnp.uint32(0)
    seen = lax.dynamic_slice(innovation, (offset, zero, zero), planes)
    coef = lax.dynamic_slice(jnp.concatenate([advect, damping[None]]), (zero, offset), (3, n)).T
    edge, far, near = call(
        edge_kernel, "edge", (1,),
        [(pos, smem()), (coef, whole((n, 3))), (edge, wh), (got_edge, wh), (seen, wn), (obs_weight, strip_spec)],
        [(halves, wh), (rows, row_spec), (rows, row_spec)],
        [pltpu.VMEM((6, n, 256), F32)],
    )
    near, far = swap_tiles(near, far)
    (grad,) = call(
        dynamics_kernel, "dynamics", (1,),
        [(pos, smem()), (advect, smem()), (damping, smem()), (edge, wh), (inner, wh),
         (got_inner, wh), (far, row_spec), (near, row_spec), (seen, wn), (obs_weight, strip_spec)],
        [((8, n, 8, 256), whole((8, n, 8, 256)))],
        [pltpu.VMEM(rows, F32)] * 2 + [pltpu.VMEM(planes, F32)],
    )
    grad = lax.all_to_all(grad, GROUP, 0, 0, tiled=True)
    send, sums = call(
        project_kernel, "project", (1,),
        [(pos, smem()), (scal, smem()), (grad, whole(grad.shape)),
         (ensemble, whole(ensemble.shape)), (loc, w2)],
        [(strip2, w2), ((32, 2, 128), whole((32, 2, 128)))],
    )
    near, far = swap_tiles(send, send)
    sums = lax.all_to_all(sums, TILE, 0, 0, tiled=True)
    cells = 32 * control.shape[1] * control.shape[2] * ensemble.shape[1]
    return tuple(
        call(
            functools.partial(end_kernel, 1.0 / math.sqrt(cells)), "end", (1,),
            [(pos, smem()), (scal, smem()), (control, w2), (send, w2), (near, w2), (far, w2),
             (sums, whole(sums.shape))],
            [(strip2, w2), ((2,), smem())],
        )
    )


def solution(mesh):
    mesh = Mesh(mesh.devices.reshape(4, 2, 2, 4, 4, 2), AXES)
    in_specs = (
        P(MEM, None, TILE, None),
        P(MEM, TILE, None),
        P(MEM),
        P(MEM),
        P(),
        P(),
        P(),
        P(None, TILE, None),
        P(TILE, None),
    )
    out_specs = (P(MEM, TILE, None), P(MEM))
    return jax.shard_map(
        per_device, mesh=mesh, in_specs=in_specs, out_specs=out_specs, check_vma=False
    )
```

```python
import functools
import math

import jax
import jax.numpy as jnp
from jax import lax
from jax.experimental import pallas as pl
from jax.experimental.pallas import tpu as pltpu
from jax.sharding import Mesh
from jax.sharding import PartitionSpec as P

SWEEPS = 8
AXES = ("x", "zp", "zq", "y", "zh", "core")
MEM = ("x", "zp", "zq")
GROUP = ("zq", "x")
TILE = ("y", "zh", "core")
F32 = jnp.float32


def smem():
    return pl.BlockSpec(memory_space=pltpu.SMEM)


def whole(shape):
    return pl.BlockSpec(shape, lambda *i: (0,) * len(shape))


def call(body, name, ins, outs, scratch=(), results=None):
    scalars, arrays = ins
    vmem = pl.BlockSpec(memory_space=pltpu.VMEM)
    return pl.pallas_call(
        body,
        in_specs=[smem() for _ in scalars] + [vmem for _ in arrays],
        out_specs=results if results else [vmem for _ in outs],
        out_shape=[jax.ShapeDtypeStruct(shape, F32) for shape in outs],
        scratch_shapes=list(scratch),
        compiler_params=pltpu.CompilerParams(vmem_limit_bytes=40 * 2**20),
        name=name,
    )(*scalars, *arrays)


def y_pair(field):
    lane = lax.broadcasted_iota(jnp.int32, field.shape, field.ndim - 1)
    last = field.shape[-1] - 1
    north = jnp.where(lane == last, 0.0, pltpu.roll(field, last, field.ndim - 1))
    south = jnp.where(lane == 0, 0.0, pltpu.roll(field, 1, field.ndim - 1))
    return north, south


def rate_of(pos, scal, m):
    rate = scal[2]
    for b in range(1, scal.shape[0] - 2):
        rate = jnp.where(pos[3 + m] == b, scal[2 + b], rate)
    return rate


def sweeps(field, rate):
    rows = field.shape[0]
    for _ in range(SWEEPS):
        north, south = y_pair(field)
        east = pltpu.roll(field, rows - 1, 0)
        west = pltpu.roll(field, 1, 0)
        field = field + rate * (east + west + north + south - 4.0 * field)
    return field[8:16]


def strips(first, own, near, far):
    above = jnp.where(first, far, near)
    below = jnp.where(first, near, far)
    return jnp.concatenate([above, own, below], axis=0)


def bring_kernel(ens, control, ens_o, control_o, sem):
    copies = [
        pltpu.make_async_copy(ens, ens_o, sem.at[0]),
        pltpu.make_async_copy(control, control_o, sem.at[1]),
    ]
    for copy in copies:
        copy.start()
    for copy in copies:
        copy.wait()


def start_kernel(pos, scal, control, far, near, ens, loc_o, part_o):
    scaled = []
    for m in range(2):
        loc = sweeps(strips(pos[0] == 0, control[m], near[m], far[m]), rate_of(pos, scal, m))
        loc_o[m] = loc
        scaled.append(scal[m] * loc)
    n = part_o.shape[1]
    for b in range(8):
        slot = lax.bitwise_xor(jnp.int32(b), pos[2])
        for j in range(0, n, 8):
            k = b * n + j
            part_o[slot, j : j + 8] = (
                ens[0, k : k + 8].astype(F32) * scaled[0][None]
                + ens[1, k : k + 8].astype(F32) * scaled[1][None]
            )


def tree(parts):
    while len(parts) > 1:
        parts = [p + q for p, q in zip(parts[::2], parts[1::2])]
    return parts[0]


def mid_kernel(parts, edge_o, inner_o):
    half = edge_o.shape[0]
    low = lax.broadcasted_iota(jnp.int32, edge_o.shape[1:], 0) < 4
    for p in range(half):
        one, two = (pltpu.roll(tree([parts[b, k] for b in range(8)]), 2, 0) for k in (p, p + half))
        edge_o[p] = jnp.where(low, one, pltpu.roll(two, 4, 0))
        inner_o[p] = jnp.where(low, pltpu.roll(one, 4, 0), two)


def edge_kernel(pos, coef, keep, got, seen, obsw, edge_o, far_o, near_o, rows):
    first = pos[0] == 0
    n = seen.shape[0]
    half = n // 2
    for p in range(half):
        edge = keep[p] + got[p]
        edge_o[p] = edge
        for j in range(4):
            row = (j + 2) % 4
            rows[row, p : p + 1] = edge[j : j + 1]
            rows[row, half + p : half + p + 1] = edge[j + 4 : j + 5]
    for p in range(n):
        rows[4, p : p + 1] = seen[p, 0:1]
        rows[5, p : p + 1] = seen[p, 7:8]
    a, b, e = coef[:, 0:1], coef[:, 1:2], coef[:, 2:3]

    def without(center, beside, sign, weight, see):
        north, south = y_pair(center)
        forward = (
            center
            - sign * a * (beside * 0.5)
            - b * ((north - south) * 0.5)
            + e * (beside + north + south - 4.0 * center)
        )
        return weight * (forward - see)

    head = (rows[0], without(rows[0], rows[1], 1.0, obsw[0:1], rows[4]), obsw[0:1])
    tail = (rows[3], without(rows[3], rows[2], -1.0, obsw[7:8], rows[5]), obsw[7:8])
    for j, (lo, hi) in enumerate(((0, n), (n, 2 * n), (2 * n, 2 * n + 1))):
        near_o[lo:hi] = jnp.where(first, tail[j], head[j])
        far_o[lo:hi] = jnp.where(first, head[j], tail[j])


def dynamics_kernel(pos, advect, damping, edge, inner, got, far, near, seen, obsw, out, above, below, inc):
    n = seen.shape[0]
    half = n // 2
    low = lax.broadcasted_iota(jnp.int32, edge.shape[1:], 0) < 4
    for p in range(half):
        outer, middle = edge[p], inner[p] + got[p]
        inc[p] = pltpu.roll(jnp.where(low, outer, pltpu.roll(middle, 4, 0)), 6, 0)
        inc[half + p] = pltpu.roll(jnp.where(low, pltpu.roll(outer, 4, 0), middle), 6, 0)
    first = pos[0] == 0
    above[...] = jnp.where(first, far[...], near[...])
    below[...] = jnp.where(first, near[...], far[...])
    weight = obsw[...]
    row = lax.broadcasted_iota(jnp.int32, weight.shape, 0)
    top, bottom = row == 0, row == weight.shape[0] - 1
    weight_above = jnp.broadcast_to(above[2 * n : 2 * n + 1], weight.shape)
    weight_below = jnp.broadcast_to(below[2 * n : 2 * n + 1], weight.shape)

    def pairs(field, over, under):
        east = jnp.where(bottom, under, pltpu.roll(field, field.shape[0] - 1, 0))
        west = jnp.where(top, over, pltpu.roll(field, 1, 0))
        north, south = y_pair(field)
        return east, west, north, south

    for p in range(n):
        k = pos[1] * n + p
        ax, ay, e = advect[0, k], advect[1, k], damping[k]
        center = inc[p]
        east, west, north, south = pairs(center, above[p : p + 1], below[p : p + 1])
        forward = (
            center
            - ax * ((east - west) * 0.5)
            - ay * ((north - south) * 0.5)
            + e * (east + west + north + south - 4.0 * center)
        )
        misfit = weight * (forward - seen[p])
        over = above[n + p : n + p + 1] + weight_above * ((e - 0.5 * ax) * center)
        under = below[n + p : n + p + 1] + weight_below * ((e + 0.5 * ax) * center)
        east, west, north, south = pairs(misfit, over, under)
        grad = (
            misfit
            + ax * ((east - west) * 0.5)
            + ay * ((north - south) * 0.5)
            + e * (east + west + north + south - 4.0 * misfit)
        )
        for b in range(8):
            out[b, p] = grad


def project_kernel(pos, scal, grad, ens, loc, send_o, sums_o):
    n = grad.shape[1]
    totals = [None, None]
    for slot in range(8):
        first = lax.bitwise_xor(jnp.int32(slot), pos[2]) * n
        for j in range(0, n, 4):
            part = grad[slot, j : j + 4]
            for m in range(2):
                more = tree([ens[m, first + j + i].astype(F32) * part[i] for i in range(4)])
                totals[m] = more if totals[m] is None else totals[m] + more
    for m in range(2):
        send_o[m] = scal[m] * totals[m]
        cells = jnp.sum(loc[m] * totals[m], axis=0, keepdims=True)
        cells = cells[:, :128] + cells[:, 128:]
        sums_o[:, m : m + 1] = jnp.broadcast_to(cells[None], (32, 1, 128))


def end_kernel(scale, pos, scal, control, send, near, far, sums, out_o, weight_o):
    for m in range(2):
        out_o[m] = control[m] + sweeps(
            strips(pos[0] == 0, send[m], near[m], far[m]), rate_of(pos, scal, m)
        )
    total = jnp.sum(sums[...], axis=0)
    for m in range(2):
        weight_o[m] = jnp.sum(total[m : m + 1]) * scale


def swap_tiles(near, far):
    n = 32
    far_pairs = [(i, (i + 1) % n if i % 2 else (i - 1) % n) for i in range(n)]
    far = lax.ppermute(far, TILE, far_pairs)
    near = lax.ppermute(near, TILE, [(i, i ^ 1) for i in range(n)])
    return near, far


def per_device(
    ensemble, control, weights, member_band, spread, advect, damping, innovation, obs_weight
):
    n = ensemble.shape[1] // 8
    ix, zp, zq, core = (lax.axis_index(a) for a in ("x", "zp", "zq", "core"))
    own = lax.bitwise_xor(zp, zq) * 4 + ix
    pos = jnp.concatenate([jnp.stack([core, own, zp * 4]).astype(jnp.int32), member_band])
    scal = jnp.concatenate([weights, spread])
    strip2, planes, rows = (2, 8, 256), (n, 8, 256), (2 * n + 1, 256)
    halves, blocks = (n // 2, 8, 256), (8, n, 8, 256)

    hbm = pl.BlockSpec(memory_space=pltpu.HBM)
    vmem = pl.BlockSpec(memory_space=pltpu.VMEM)
    ens, own_control = pl.pallas_call(
        bring_kernel,
        in_specs=[hbm, hbm],
        out_specs=[vmem, vmem],
        out_shape=[jax.ShapeDtypeStruct(a.shape, a.dtype) for a in (ensemble, control)],
        scratch_shapes=[pltpu.SemaphoreType.DMA((2,))],
        compiler_params=pltpu.CompilerParams(vmem_limit_bytes=40 * 2**20),
        name="bring",
    )(ensemble, control)
    near0, far0 = swap_tiles(control, control)
    loc, parts = call(
        start_kernel, "start", ([pos, scal], [own_control, far0, near0, ens]), [strip2, blocks]
    )
    parts, offset = lax.optimization_barrier((parts, (own * n).astype(jnp.uint32)))
    parts = lax.all_to_all(parts, GROUP, 0, 0, tiled=True)
    edge, inner = call(mid_kernel, "mid", ([], [parts]), [halves, halves])
    across = [(0, 3), (3, 0), (1, 2), (2, 1)]
    got_edge = lax.ppermute(edge, ("zp", "zq"), across)
    got_inner = lax.ppermute(inner, ("zp", "zq"), across)
    zero = jnp.uint32(0)
    seen = lax.dynamic_slice(innovation, (offset, zero, zero), planes)
    coef = lax.dynamic_slice(jnp.concatenate([advect, damping[None]]), (zero, offset), (3, n)).T
    edge, far, near = call(
        edge_kernel, "edge", ([pos], [coef, edge, got_edge, seen, obs_weight]),
        [halves, rows, rows], [pltpu.VMEM((6, n, 256), F32)],
    )
    near, far = swap_tiles(near, far)
    (grad,) = call(
        dynamics_kernel, "dynamics",
        ([pos, advect, damping], [edge, inner, got_inner, far, near, seen, obs_weight]),
        [blocks], [pltpu.VMEM(rows, F32)] * 2 + [pltpu.VMEM(planes, F32)],
    )
    grad = lax.all_to_all(grad, GROUP, 0, 0, tiled=True)
    send, sums = call(
        project_kernel, "project", ([pos, scal], [grad, ensemble, loc]), [strip2, (32, 2, 128)]
    )
    near, far = swap_tiles(send, send)
    sums = lax.all_to_all(sums, TILE, 0, 0, tiled=True)
    cells = 32 * control.shape[1] * control.shape[2] * ensemble.shape[1]
    return tuple(
        pl.pallas_call(
            functools.partial(end_kernel, 1.0 / math.sqrt(cells)),
            grid=(1,),
            in_specs=[smem(), smem()] + [whole(strip2)] * 4 + [whole(sums.shape)],
            out_specs=[whole(strip2), smem()],
            out_shape=[jax.ShapeDtypeStruct(strip2, F32), jax.ShapeDtypeStruct((2,), F32)],
            compiler_params=pltpu.CompilerParams(vmem_limit_bytes=40 * 2**20),
            name="end",
        )(pos, scal, control, send, near, far, sums)
    )


def solution(mesh):
    mesh = Mesh(mesh.devices.reshape(4, 2, 2, 4, 4, 2), AXES)
    in_specs = (
        P(MEM, None, TILE, None),
        P(MEM, TILE, None),
        P(MEM),
        P(MEM),
        P(),
        P(),
        P(),
        P(None, TILE, None),
        P(TILE, None),
    )
    out_specs = (P(MEM, TILE, None), P(MEM))
    return jax.shard_map(
        per_device, mesh=mesh, in_specs=in_specs, out_specs=out_specs, check_vma=False
    )
```

```python
import functools
import math

import jax
import jax.numpy as jnp
from jax import lax
from jax.experimental import pallas as pl
from jax.experimental.pallas import tpu as pltpu
from jax.sharding import Mesh
from jax.sharding import PartitionSpec as P

SWEEPS = 8
AXES = ("x", "zp", "zq", "y", "zh", "core")
MEM = ("x", "zp", "zq")
GROUP = ("zq", "x")
TILE = ("y", "zh", "core")
F32 = jnp.float32


def smem():
    return pl.BlockSpec(memory_space=pltpu.SMEM)


def whole(shape):
    return pl.BlockSpec(shape, lambda *i: (0,) * len(shape))


def call(body, name, ins, outs, scratch=(), results=None):
    scalars, arrays = ins
    vmem = pl.BlockSpec(memory_space=pltpu.VMEM)
    return pl.pallas_call(
        body,
        in_specs=[smem() for _ in scalars] + [vmem for _ in arrays],
        out_specs=results if results else [vmem for _ in outs],
        out_shape=[jax.ShapeDtypeStruct(shape, F32) for shape in outs],
        scratch_shapes=list(scratch),
        compiler_params=pltpu.CompilerParams(vmem_limit_bytes=40 * 2**20),
        name=name,
    )(*scalars, *arrays)


def y_pair(field):
    lane = lax.broadcasted_iota(jnp.int32, field.shape, field.ndim - 1)
    last = field.shape[-1] - 1
    north = jnp.where(lane == last, 0.0, pltpu.roll(field, last, field.ndim - 1))
    south = jnp.where(lane == 0, 0.0, pltpu.roll(field, 1, field.ndim - 1))
    return north, south


def rate_of(band, scal, m):
    rate = scal[2]
    for b in range(1, scal.shape[0] - 2):
        rate = jnp.where(band[m] == b, scal[2 + b], rate)
    return rate


def sweeps(field, rate):
    rows = field.shape[0]
    for _ in range(SWEEPS):
        north, south = y_pair(field)
        east = pltpu.roll(field, rows - 1, 0)
        west = pltpu.roll(field, 1, 0)
        field = field + rate * (east + west + north + south - 4.0 * field)
    return field[8:16]


def strips(first, own, near, far):
    above = jnp.where(first, far, near)
    below = jnp.where(first, near, far)
    return jnp.concatenate([above, own, below], axis=0)


def bring_kernel(ens, control, ens_o, control_o, sem):
    copies = [
        pltpu.make_async_copy(ens, ens_o, sem.at[0]),
        pltpu.make_async_copy(control, control_o, sem.at[1]),
    ]
    for copy in copies:
        copy.start()
    for copy in copies:
        copy.wait()


def start_kernel(pos, band, scal, control, far, near, ens, loc_o, part_o):
    scaled = []
    for m in range(2):
        loc = sweeps(strips(pos[0] == 0, control[m], near[m], far[m]), rate_of(band, scal, m))
        loc_o[m] = loc
        scaled.append(scal[m] * loc)
    n = part_o.shape[1]
    for b in range(8):
        slot = lax.bitwise_xor(jnp.int32(b), pos[2])
        for j in range(0, n, 8):
            k = b * n + j
            part_o[slot, j : j + 8] = (
                ens[0, k : k + 8].astype(F32) * scaled[0][None]
                + ens[1, k : k + 8].astype(F32) * scaled[1][None]
            )


def tree(parts):
    while len(parts) > 1:
        parts = [p + q for p, q in zip(parts[::2], parts[1::2])]
    return parts[0]


def mid_kernel(parts, edge_o, inner_o):
    half = edge_o.shape[0]
    low = lax.broadcasted_iota(jnp.int32, edge_o.shape[1:], 0) < 4
    for p in range(half):
        one, two = (pltpu.roll(tree([parts[b, k] for b in range(8)]), 2, 0) for k in (p, p + half))
        edge_o[p] = jnp.where(low, one, pltpu.roll(two, 4, 0))
        inner_o[p] = jnp.where(low, pltpu.roll(one, 4, 0), two)


def edge_kernel(pos, coef, keep, got, seen, obsw, edge_o, far_o, near_o, rows):
    first = pos[0] == 0
    n = seen.shape[0]
    half = n // 2
    for p in range(half):
        edge = keep[p] + got[p]
        edge_o[p] = edge
        for j in range(4):
            row = (j + 2) % 4
            rows[row, p : p + 1] = edge[j : j + 1]
            rows[row, half + p : half + p + 1] = edge[j + 4 : j + 5]
    for p in range(n):
        rows[4, p : p + 1] = seen[p, 0:1]
        rows[5, p : p + 1] = seen[p, 7:8]
    a, b, e = coef[:, 0:1], coef[:, 1:2], coef[:, 2:3]

    def without(center, beside, sign, weight, see):
        north, south = y_pair(center)
        forward = (
            center
            - sign * a * (beside * 0.5)
            - b * ((north - south) * 0.5)
            + e * (beside + north + south - 4.0 * center)
        )
        return weight * (forward - see)

    head = (rows[0], without(rows[0], rows[1], 1.0, obsw[0:1], rows[4]), obsw[0:1])
    tail = (rows[3], without(rows[3], rows[2], -1.0, obsw[7:8], rows[5]), obsw[7:8])
    for j, (lo, hi) in enumerate(((0, n), (n, 2 * n), (2 * n, 2 * n + 1))):
        near_o[lo:hi] = jnp.where(first, tail[j], head[j])
        far_o[lo:hi] = jnp.where(first, head[j], tail[j])


def dynamics_kernel(pos, advect, damping, edge, inner, got, far, near, seen, obsw, out, above, below, inc):
    n = seen.shape[0]
    half = n // 2
    low = lax.broadcasted_iota(jnp.int32, edge.shape[1:], 0) < 4
    for p in range(half):
        outer, middle = edge[p], inner[p] + got[p]
        inc[p] = pltpu.roll(jnp.where(low, outer, pltpu.roll(middle, 4, 0)), 6, 0)
        inc[half + p] = pltpu.roll(jnp.where(low, pltpu.roll(outer, 4, 0), middle), 6, 0)
    first = pos[0] == 0
    above[...] = jnp.where(first, far[...], near[...])
    below[...] = jnp.where(first, near[...], far[...])
    weight = obsw[...]
    row = lax.broadcasted_iota(jnp.int32, weight.shape, 0)
    top, bottom = row == 0, row == weight.shape[0] - 1
    weight_above = jnp.broadcast_to(above[2 * n : 2 * n + 1], weight.shape)
    weight_below = jnp.broadcast_to(below[2 * n : 2 * n + 1], weight.shape)

    def pairs(field, over, under):
        east = jnp.where(bottom, under, pltpu.roll(field, field.shape[0] - 1, 0))
        west = jnp.where(top, over, pltpu.roll(field, 1, 0))
        north, south = y_pair(field)
        return east, west, north, south

    for p in range(n):
        k = pos[1] * n + p
        ax, ay, e = advect[0, k], advect[1, k], damping[k]
        center = inc[p]
        east, west, north, south = pairs(center, above[p : p + 1], below[p : p + 1])
        forward = (
            center
            - ax * ((east - west) * 0.5)
            - ay * ((north - south) * 0.5)
            + e * (east + west + north + south - 4.0 * center)
        )
        misfit = weight * (forward - seen[p])
        over = above[n + p : n + p + 1] + weight_above * ((e - 0.5 * ax) * center)
        under = below[n + p : n + p + 1] + weight_below * ((e + 0.5 * ax) * center)
        east, west, north, south = pairs(misfit, over, under)
        grad = (
            misfit
            + ax * ((east - west) * 0.5)
            + ay * ((north - south) * 0.5)
            + e * (east + west + north + south - 4.0 * misfit)
        )
        for b in range(8):
            out[b, p] = grad


def project_kernel(pos, scal, grad, ens, loc, send_o, sums_o):
    n = grad.shape[1]
    totals = [None, None]
    for slot in range(8):
        first = lax.bitwise_xor(jnp.int32(slot), pos[2]) * n
        for j in range(0, n, 4):
            part = grad[slot, j : j + 4]
            for m in range(2):
                more = tree([ens[m, first + j + i].astype(F32) * part[i] for i in range(4)])
                totals[m] = more if totals[m] is None else totals[m] + more
    for m in range(2):
        send_o[m] = scal[m] * totals[m]
        cells = jnp.sum(loc[m] * totals[m], axis=0, keepdims=True)
        cells = cells[:, :128] + cells[:, 128:]
        sums_o[:, m : m + 1] = jnp.broadcast_to(cells[None], (32, 1, 128))


def end_kernel(scale, pos, band, scal, control, send, near, far, sums, out_o, weight_o):
    for m in range(2):
        out_o[m] = control[m] + sweeps(
            strips(pos[0] == 0, send[m], near[m], far[m]), rate_of(band, scal, m)
        )
    total = jnp.sum(sums[...], axis=0)
    for m in range(2):
        weight_o[m] = jnp.sum(total[m : m + 1]) * scale


def swap_tiles(near, far):
    n = 32
    far_pairs = [(i, (i + 1) % n if i % 2 else (i - 1) % n) for i in range(n)]
    far = lax.ppermute(far, TILE, far_pairs)
    near = lax.ppermute(near, TILE, [(i, i ^ 1) for i in range(n)])
    return near, far


def per_device(
    ensemble, control, weights, member_band, spread, advect, damping, innovation, obs_weight
):
    n = ensemble.shape[1] // 8
    ix, zp, zq, core = (lax.axis_index(a) for a in ("x", "zp", "zq", "core"))
    own = lax.bitwise_xor(zp, zq) * 4 + ix
    pos = jnp.stack([core, own, zp * 4]).astype(jnp.int32)
    scal = jnp.concatenate([weights, spread])
    strip2, planes, rows = (2, 8, 256), (n, 8, 256), (2 * n + 1, 256)
    halves, blocks = (n // 2, 8, 256), (8, n, 8, 256)

    hbm = pl.BlockSpec(memory_space=pltpu.HBM)
    vmem = pl.BlockSpec(memory_space=pltpu.VMEM)
    ens, own_control = pl.pallas_call(
        bring_kernel,
        in_specs=[hbm, hbm],
        out_specs=[vmem, vmem],
        out_shape=[jax.ShapeDtypeStruct(a.shape, a.dtype) for a in (ensemble, control)],
        scratch_shapes=[pltpu.SemaphoreType.DMA((2,))],
        compiler_params=pltpu.CompilerParams(vmem_limit_bytes=40 * 2**20),
        name="bring",
    )(ensemble, control)
    near0, far0 = swap_tiles(control, control)
    loc, parts = call(
        start_kernel, "start", ([pos, member_band, scal], [own_control, far0, near0, ens]), [strip2, blocks]
    )
    parts, offset = lax.optimization_barrier((parts, (own * n).astype(jnp.uint32)))
    parts = lax.all_to_all(parts, GROUP, 0, 0, tiled=True)
    edge, inner = call(mid_kernel, "mid", ([], [parts]), [halves, halves])
    across = [(0, 3), (3, 0), (1, 2), (2, 1)]
    got_edge = lax.ppermute(edge, ("zp", "zq"), across)
    got_inner = lax.ppermute(inner, ("zp", "zq"), across)
    zero = jnp.uint32(0)
    seen = lax.dynamic_slice(innovation, (offset, zero, zero), planes)
    coef = lax.dynamic_slice(jnp.concatenate([advect, damping[None]]), (zero, offset), (3, n)).T
    edge, far, near = call(
        edge_kernel, "edge", ([pos], [coef, edge, got_edge, seen, obs_weight]),
        [halves, rows, rows], [pltpu.VMEM((6, n, 256), F32)],
    )
    near, far = swap_tiles(near, far)
    (grad,) = call(
        dynamics_kernel, "dynamics",
        ([pos, advect, damping], [edge, inner, got_inner, far, near, seen, obs_weight]),
        [blocks], [pltpu.VMEM(rows, F32)] * 2 + [pltpu.VMEM(planes, F32)],
    )
    grad = lax.all_to_all(grad, GROUP, 0, 0, tiled=True)
    send, sums = call(
        project_kernel, "project", ([pos, scal], [grad, ensemble, loc]), [strip2, (32, 2, 128)]
    )
    near, far = swap_tiles(send, send)
    sums = lax.all_to_all(sums, TILE, 0, 0, tiled=True)
    cells = 32 * control.shape[1] * control.shape[2] * ensemble.shape[1]
    return tuple(
        pl.pallas_call(
            functools.partial(end_kernel, 1.0 / math.sqrt(cells)),
            grid=(1,),
            in_specs=[smem(), smem(), smem()] + [whole(strip2)] * 4 + [whole(sums.shape)],
            out_specs=[whole(strip2), smem()],
            out_shape=[jax.ShapeDtypeStruct(strip2, F32), jax.ShapeDtypeStruct((2,), F32)],
            compiler_params=pltpu.CompilerParams(vmem_limit_bytes=40 * 2**20),
            name="end",
        )(pos, member_band, scal, control, send, near, far, sums)
    )


def solution(mesh):
    mesh = Mesh(mesh.devices.reshape(4, 2, 2, 4, 4, 2), AXES)
    in_specs = (
        P(MEM, None, TILE, None),
        P(MEM, TILE, None),
        P(MEM),
        P(MEM),
        P(),
        P(),
        P(),
        P(None, TILE, None),
        P(TILE, None),
    )
    out_specs = (P(MEM, TILE, None), P(MEM))
    return jax.shard_map(
        per_device, mesh=mesh, in_specs=in_specs, out_specs=out_specs, check_vma=False
    )
```
